256 devices in a mesh: blk: 64 (over z, y_hi, x), rep: 4 (over y_lo, core).
Axes of the slice: x: 4, y: 4 (y_hi: 2, y_lo: 2; y = y_hi * 2 + y_lo), z: 8, core: 2. Of those that a mesh axis runs over, the one named last changes fastest.
Arguments:
- features: bfloat16 [131072, 512], P('blk', 'rep'), may hold values from -6 to 6
- order: int32 [1024, 128], P('blk'), may hold values from 0 to 127, each once within a row
- columns: int32 [1024, 16], P('blk'), may hold values from 0 to 1023, as said below
- tiles: bfloat16 [1024, 16, 128, 128], P('blk'), may hold values from -0.125 to 0.125
- w_rel: bfloat16 [512, 512], P(None, 'rep'), may hold values from -0.25 to 0.25
- w_root: bfloat16 [512, 512], P(None, 'rep'), may hold values from -0.25 to 0.25
- upstream: bfloat16 [131072, 512], P('blk', 'rep'), may hold values from -6 to 6
Outputs:
- hidden: bfloat16 [131072, 512], P('blk', 'rep')
- grad_features: bfloat16 [131072, 512], P('blk', 'rep')
- grad_rel: float32 [512, 512], P(None, 'rep')
- grad_root: float32 [512, 512], P(None, 'rep')
The draws below stay inside these ranges and needn't reach their ends.
Inputs may be any that keep to these rules, and one draw needn't show every extreme that they name: `order`: each row holds every number below 128 once. `columns`: blocks form groups of 16 consecutive blocks on a closed loop of 1024 / 16 groups; a block-row's 16 column blocks are distinct, include its own block, and lie in groups at most 3 steps from its own group along the loop; every block-row has one column block exactly 3 groups ahead and one exactly 3 groups behind.
All inputs are finite; a program needn't handle non-finite values.
Results may differ from the reference program's by a relative error of at most 0.015.
Values may be sent and summed in bfloat16 or wider, within the bound.
A program may use at most 128 MiB of HBM per device.

```python
import jax
import jax.numpy as jnp
from jax import lax

F = 512
BS = 128
NNZ = 16
REACH = 3
BG = 16
NB = 1024
NODES = 131072


def draw_columns(key, part):
    key = jax.random.fold_in(key, 11)
    span_len = 2 * REACH + 1
    candidates = span_len * BG
    groups_total = NB // BG
    key_scores, key_ahead, key_behind = jax.random.split(key, 3)
    cand_ids = jnp.arange(candidates, dtype=jnp.int32)[None, :]
    scores = jax.random.randint(key_scores, (NB, candidates), 0, 2 ** 20, dtype=jnp.int32) * candidates + cand_ids
    block_ids = jnp.arange(NB, dtype=jnp.int32)
    ahead_pick = jax.random.randint(key_ahead, (NB,), 0, BG, dtype=jnp.int32) + (span_len - 1) * BG
    behind_pick = jax.random.randint(key_behind, (NB,), 0, BG, dtype=jnp.int32)
    self_pick = REACH * BG + block_ids % BG
    forced = (cand_ids == ahead_pick[:, None]) | (cand_ids == behind_pick[:, None]) | (cand_ids == self_pick[:, None])
    scores = scores + forced.astype(jnp.int32) * 2 ** 28
    _, chosen = lax.top_k(scores, NNZ)
    offset_index = chosen // BG
    local_index = chosen % BG
    target_group = (block_ids[:, None] // BG + offset_index - REACH) % groups_total
    return (target_group * BG + local_index).astype(jnp.int32)


def steps_of(key, shape, cuts, low, high):
    def one(axis_at, blocks):
        steps = jax.random.uniform(jax.random.fold_in(jax.random.fold_in(key, 6), axis_at), (blocks,), jnp.float32, low / len(cuts), high / len(cuts))
        return jnp.repeat(jnp.exp(steps), shape[axis_at] // blocks).reshape((-1,) + (1,) * (len(shape) - axis_at - 1))

    loudness = one(*cuts[0])
    for cut in cuts[1:]:
        loudness = loudness * one(*cut)
    return loudness


def noise(own_key, extent, width, bound, shards=(), held_as=jnp.bfloat16):
    factor_of = steps_of(own_key, extent, shards, -0.22, 0.18) if shards else 1.0
    values = jax.random.normal(own_key, extent, jnp.float32) * width * factor_of
    return jnp.minimum(jnp.maximum(values, -bound), bound).astype(held_as)


def setup_inputs(seed: int = 0) -> dict:
    splits = jax.random.split(jax.random.key(seed), 8)
    features = noise(splits[0], (NODES, F), 1.0, 6.0, ((0, 64), (1, 4)))
    order = jax.vmap(lambda own: jax.random.permutation(own, BS))(jax.random.split(splits[1], NB)).reshape((NB, BS)).astype(jnp.int32)
    columns = draw_columns(jax.random.fold_in(splits[7], 71), 0)
    tiles = noise(splits[3], (NB, NNZ, BS, BS), (NNZ * BS) ** -0.5, 0.125, ((0, 64),))
    w_rel = noise(splits[4], (F, F), F ** -0.5, 0.25, ((1, 4),))
    w_root = noise(splits[5], (F, F), F ** -0.5, 0.25, ((1, 4),))
    upstream = noise(splits[6], (NODES, F), 1.0, 6.0, ((0, 64), (1, 4)))
    return dict(features=features, order=order, columns=columns, tiles=tiles, w_rel=w_rel, w_root=w_root, upstream=upstream)


def activate(values):
    return jax.nn.gelu(values, approximate=True)

def reference(features, order, columns, tiles, w_rel, w_root, upstream):
    ordered = jnp.take_along_axis(features.reshape(NB, BS, F), order[:, :, None], axis=1)
    group_count = NB // BG

    def aggregate_group(group_idx):
        col_ids = lax.dynamic_slice_in_dim(columns, group_idx * BG, BG, 0)
        tile_rows = lax.dynamic_slice_in_dim(tiles, group_idx * BG, BG, 0)
        sources = ordered[col_ids]
        summed = jnp.einsum('bkij,bkjf->bif', tile_rows.astype(jnp.float32), sources.astype(jnp.float32))
        return summed.astype(jnp.bfloat16)
    aggregated = lax.map(aggregate_group, jnp.arange(group_count, dtype=jnp.int32)).reshape(NODES, F)
    ordered_rows = ordered.reshape(NODES, F)
    preact = jnp.dot(aggregated, w_rel, preferred_element_type=jnp.float32) + jnp.dot(ordered_rows, w_root, preferred_element_type=jnp.float32)
    activated, pull_back = jax.vjp(activate, preact)
    hidden = activated.astype(jnp.bfloat16)
    grad_pre = pull_back(upstream.astype(jnp.float32))[0].astype(jnp.bfloat16)
    grad_rel = jnp.dot(aggregated.T, grad_pre, preferred_element_type=jnp.float32)
    grad_root = jnp.dot(ordered_rows.T, grad_pre, preferred_element_type=jnp.float32)
    grad_agg = jnp.dot(grad_pre, w_rel.T, preferred_element_type=jnp.float32).astype(jnp.bfloat16).reshape(NB, BS, F)
    root_back = jnp.dot(grad_pre, w_root.T, preferred_element_type=jnp.float32)

    def push_group(accum_back, group_idx):
        col_ids = lax.dynamic_slice_in_dim(columns, group_idx * BG, BG, 0)
        tile_rows = lax.dynamic_slice_in_dim(tiles, group_idx * BG, BG, 0)
        grad_block = lax.dynamic_slice_in_dim(grad_agg, group_idx * BG, BG, 0)
        contrib = jnp.einsum('bkji,bjf->bkif', tile_rows.astype(jnp.float32), grad_block.astype(jnp.float32))
        accum_back = accum_back.at[col_ids.reshape(-1)].add(contrib.reshape(BG * NNZ, BS, F))
        return (accum_back, None)
    accum_back, _ = lax.scan(push_group, jnp.zeros((NB, BS, F), jnp.float32), jnp.arange(group_count, dtype=jnp.int32))
    grad_ordered = (accum_back.reshape(NODES, F) + root_back).astype(jnp.bfloat16).reshape(NB, BS, F)
    inverse = jnp.argsort(order, axis=1).astype(jnp.int32)
    grad_features = jnp.take_along_axis(grad_ordered, inverse[:, :, None], axis=1).reshape(NODES, F)
    return (hidden, grad_features, grad_rel, grad_root)
```

```python
import jax
import jax.numpy as jnp
from jax import lax
from jax.experimental import pallas as pl
from jax.experimental.pallas import tpu as pltpu
from jax.sharding import PartitionSpec as P

MESH = pl.DeviceIdType.MESH
REACH = 3
SPAN = 2 * REACH + 1
ROW = 4
HALO_CHUNKS = 8
MID_CHUNKS = 8
BACK_CHUNKS = 8
BF = jnp.bfloat16
F32 = jnp.float32
NT = (((1,), (1,)), ((), ()))
TN = (((0,), (0,)), ((), ()))
MIB = 2**20


class Place:
    def __init__(self, groups):
        blk = lax.axis_index("blk")
        rep = lax.axis_index("rep")
        self.groups = groups
        self.rows = groups // ROW
        self.blk, self.rep = blk, rep
        x = lax.rem(blk, ROW)
        self.x = x
        self.row = lax.div(blk, ROW)
        half, odd = lax.div(x, 2), lax.rem(x, 2)
        self.n1 = 3 - x
        self.n2 = x + 1 - 2 * odd
        self.diag = lax.rem(x + 2, 4)
        self.step_p = 1 - 2 * half
        self.step_q = 1 - 2 * odd
        self.slot_n1 = REACH + self.n1 - x
        self.slot_n2 = REACH + self.n2 - x
        self.slot_diag = REACH + self.diag - x
        self.slot_p = REACH + self.n1 - x - ROW * self.step_p
        self.slot_q = REACH + self.n2 - x - ROW * self.step_q
        self.slot_post = 1 + 4 * half
        self.core = lax.rem(rep, 2)
        self.low = lax.div(rep, 2)
        self.rep_sib = 2 * self.low + 1 - self.core
        self.rep_y = 2 * (1 - self.low) + self.core
        self.rep_far = 2 * (1 - self.low) + 1 - self.core

    def at_x(self, x):
        return (self.row * ROW + x, self.rep)

    def at_row(self, row):
        return (row * ROW + self.x, self.rep)

    def row_by(self, step):
        return self.at_row(lax.rem(self.row + step + self.rows, self.rows))

    def at_rep(self, rep):
        return (self.blk, rep)


def greet(partners):
    barrier = pltpu.get_barrier_semaphore()
    for who in partners:
        pl.semaphore_signal(barrier, inc=1, device_id=who, device_id_type=MESH)
    pl.semaphore_wait(barrier, len(partners))


def remote(src, dst, send, recv, who):
    return pltpu.make_async_remote_copy(
        src_ref=src, dst_ref=dst, send_sem=send, recv_sem=recv, device_id=who, device_id_type=MESH
    )


def onehot(order_ref, b):
    length = order_ref.shape[1]
    node = lax.broadcasted_iota(jnp.int32, (length, length), 0)
    return (node == order_ref[pl.ds(b, 1), :]).astype(F32).astype(BF)


def slot_of(col, place, blocks):
    group = lax.div(col, blocks)
    offset = lax.rem(group - place.blk + REACH + place.groups, place.groups)
    return lax.min(offset, SPAN - 1) * blocks + lax.rem(col, blocks)


def forward_kernel(
    groups,
    cols, feat, order, tiles, w_rel, w_root, upstream,
    hidden, back_agg, back_root, wgrad,
    win, tbuf, agg, slab, keep, s1, r1, s2, r2, pre,
    tile_sem, hs, hr, ws, wr, ms, mr,
):
    me = Place(groups)
    blocks, bl, width = feat.shape
    per_row = cols.shape[1]
    own = REACH * blocks
    nc = HALO_CHUNKS
    hb = blocks // nc
    nm = MID_CHUNKS
    mb = blocks // nm
    mrows = mb * bl

    tile_copy = pltpu.make_async_copy(tiles, tbuf, tile_sem)
    tile_copy.start()
    sib, far_y, far = me.at_rep(me.rep_sib), me.at_rep(me.rep_y), me.at_rep(me.rep_far)
    greet([me.at_x(me.n1), me.at_x(me.n2), me.row_by(1), me.row_by(-1), sib, far_y, far])

    def halo(kind, c):
        src_slot, dst_slot, who = [
            (REACH, REACH + me.x - me.n1, me.at_x(me.n1)),
            (REACH, REACH + me.x - me.n2, me.at_x(me.n2)),
            (me.slot_n2, REACH + me.n2 - me.n1, me.at_x(me.n1)),
            (me.slot_n1, me.slot_p, me.row_by(me.step_p)),
            (me.slot_n2, me.slot_q, me.row_by(me.step_q)),
            (me.slot_p, me.slot_post, me.at_x(me.n2)),
        ][kind]
        return remote(
            win.at[pl.ds(src_slot * blocks + c * hb, hb)],
            win.at[pl.ds(dst_slot * blocks + c * hb, hb)],
            hs.at[kind, c], hr.at[kind, c], who,
        )

    @pl.loop(0, nc)
    def _(c):
        for i in range(hb):
            b = c * hb + i
            win[own + b] = lax.dot_general(
                onehot(order, b), feat[b], TN, preferred_element_type=F32
            ).astype(BF)
        halo(0, c).start()
        halo(1, c).start()

    def weight(i, j):
        who = (me.rep_sib, me.rep_y, me.rep_far)[i]
        src = (w_rel, w_root)[j]
        return remote(
            src.at[pl.ds(who * width, width)], slab.at[me.rep, pl.ds(j * width, width)],
            ws.at[i, j], wr.at[i, j], me.at_rep(who),
        )

    for i in range(3):
        for j in range(2):
            weight(i, j).start()
    for j, src in enumerate((w_rel, w_root)):
        slab[me.rep, j * width : (j + 1) * width] = src[pl.ds(me.rep * width, width), :]

    @pl.loop(0, nc + 2)
    def _(s):
        @pl.when(s < nc)
        def _():
            halo(0, s).wait_recv()
            halo(1, s).wait_recv()
            halo(2, s).start()
            halo(3, s).start()
            halo(4, s).start()

        @pl.when(s >= 2)
        def _():
            halo(3, s - 2).wait_recv()
            halo(5, s - 2).start()

    @pl.loop(0, nc)
    def _(c):
        for kind in (2, 4, 5):
            halo(kind, c).wait_recv()

    for i in range(3):
        for j in range(2):
            weight(i, j).wait_recv()
    tile_copy.wait()

    panel_sib = [2 * (1 - me.low) + 1 - me.core, 2 * me.low + 1 - me.core]
    panel_mine = [me.rep_y, me.rep]

    def rows(c):
        return pl.ds(c * mb, mb)

    def mid(kind, c):
        src, dst, who = [
            (s1.at[c], r1.at[c], sib),
            (s2.at[c], r2.at[c], far_y),
            (pre.at[me.rep, rows(c)], pre.at[me.rep, rows(c)], far_y),
            (pre.at[me.rep, rows(c)], pre.at[me.rep, rows(c)], sib),
            (pre.at[me.rep_y, rows(c)], pre.at[me.rep_y, rows(c)], sib),
        ][kind]
        return remote(src, dst, ms.at[kind, c], mr.at[kind, c], who)

    def both(c):
        return jnp.concatenate(
            [
                agg[rows(c)].reshape(mrows, width),
                win[pl.ds(own + c * mb, mb)].reshape(mrows, width),
            ],
            axis=1,
        )

    @pl.loop(0, nm + 4)
    def _(s):
        @pl.when(s < nm)
        def _():
            for i in range(mb):
                b = s * mb + i
                left = jnp.concatenate([tbuf[b, k] for k in range(per_row)], axis=1)
                right = jnp.concatenate(
                    [win[slot_of(cols[b, k], me, blocks)] for k in range(per_row)], axis=0
                )
                agg[b] = jnp.dot(left, right, preferred_element_type=F32).astype(BF)
            x = both(s)
            for i in range(2):
                part = jnp.dot(x, slab[panel_sib[i]], preferred_element_type=F32)
                s1[s, i] = part.astype(BF)
            mid(0, s).start()
            for i in range(2):
                keep[s, i] = jnp.dot(x, slab[panel_mine[i]], preferred_element_type=F32)

        @pl.when((s >= 1) & (s < nm + 1))
        def _():
            c = s - 1
            mid(0, c).wait_recv()
            s2[c] = (keep[c, 0] + r1[c, 0].astype(F32)).astype(BF)
            mid(1, c).start()

        @pl.when((s >= 2) & (s < nm + 2))
        def _():
            c = s - 2
            mid(1, c).wait_recv()
            v = keep[c, 1] + r1[c, 1].astype(F32) + r2[c].astype(F32)
            sq = v * v
            t = jnp.tanh(0.7978845608 * (v + 0.044715 * (sq * v)))
            up = upstream[rows(c)].reshape(mrows, width).astype(F32)
            hidden[rows(c)] = (0.5 * v * (1.0 + t)).astype(BF).reshape(mb, bl, width)
            slope = 0.5 * (1.0 + t) + 0.5 * v * (1.0 - t * t) * (
                0.7978845608 * (1.0 + 0.134145 * sq)
            )
            pre[me.rep, rows(c)] = (up * slope).astype(BF).reshape(mb, bl, width)
            mid(2, c).start()
            mid(3, c).start()

        @pl.when((s >= 3) & (s < nm + 3))
        def _():
            mid(2, s - 3).wait_recv()
            mid(4, s - 3).start()

        @pl.when(s >= 4)
        def _():
            c = s - 4
            mid(3, c).wait_recv()
            mid(4, c).wait_recv()
            x = both(c)
            gathered = jnp.concatenate(
                [pre[p, rows(c)].reshape(mrows, width) for p in range(4)], axis=1
            )
            slabs = jnp.concatenate([slab[p] for p in range(4)], axis=1)
            back = lax.dot_general(slabs, gathered, NT, preferred_element_type=F32)
            for i in range(mb):
                cut = back[:, i * bl : (i + 1) * bl]
                back_agg[c * mb + i] = cut[:width].astype(BF)
                back_root[c * mb + i] = cut[width:]
            grads = lax.dot_general(x, gathered, TN, preferred_element_type=F32)

            @pl.when(c == 0)
            def _():
                for p in range(4):
                    wgrad[p] = grads[:, p * width : (p + 1) * width]

            @pl.when(c > 0)
            def _():
                for p in range(4):
                    wgrad[p] += grads[:, p * width : (p + 1) * width]

    @pl.loop(0, nc)
    def _(c):
        for kind in range(6):
            halo(kind, c).wait_send()

    @pl.loop(0, nm)
    def _(c):
        for kind in range(5):
            mid(kind, c).wait_send()

    for i in range(3):
        for j in range(2):
            weight(i, j).wait_send()


def push_kernel(groups, cols, tiles, back_agg, sums, own_sums, acc):
    me = Place(groups)
    b = pl.program_id(0)
    steps, per_row = cols.shape
    blocks = steps

    @pl.when(b == 0)
    def _():
        acc[...] = jnp.zeros_like(acc)

    right = jnp.concatenate([tiles[0, k] for k in range(per_row)], axis=1)
    res = jnp.dot(back_agg[0], right, preferred_element_type=F32)
    bl = tiles.shape[-1]
    for k in range(per_row):
        acc[slot_of(cols[b, k], me, blocks)] += res[:, k * bl : (k + 1) * bl]

    @pl.when(b == steps - 1)
    def _():
        @pl.loop(0, acc.shape[0])
        def _(s):
            sums[s] = acc[s].astype(BF)

        @pl.loop(0, blocks)
        def _(s):
            own_sums[s] = acc[REACH * blocks + s]


def backward_kernel(
    groups,
    sums, own_sums, back_root, order, wgrad,
    grad_feat, grad_rel, grad_root,
    land, out, wsend, a0, a1, a2, a3, a4, piece, done,
    hs, hr, e0s, e0r, e1s, e1r, e2s, e2r, e3s, e3r, e4s, e4r,
):
    me = Place(groups)
    blocks, bl = order.shape
    width = own_sums.shape[1]
    nc = BACK_CHUNKS
    hb = blocks // nc
    rows = me.rows
    x_others = [me.n1, me.n2, me.diag]
    rep_others = [me.rep_sib, me.rep_y, me.rep_far]
    greet(
        [me.at_x(x) for x in x_others]
        + [me.at_rep(r) for r in rep_others]
        + [me.row_by(d) for d in range(1, rows)]
    )

    POST, DIAG, Q, PP, N2, N1 = range(6)

    def part(ref, slot, c):
        return ref.at[pl.ds(slot * blocks + c * hb, hb)]

    def halo(kind, c):
        src, who = [
            (part(sums, me.slot_post, c), me.at_x(me.n2)),
            (part(sums, me.slot_diag, c), me.at_x(me.n1)),
            (part(sums, me.slot_q, c), me.row_by(-me.step_q)),
            (part(out, 0, c), me.row_by(-me.step_p)),
            (part(out, 1, c), me.at_x(me.n2)),
            (part(out, 2, c), me.at_x(me.n1)),
        ][kind]
        return remote(src, part(land, kind, c), hs.at[kind, c], hr.at[kind, c], who)

    def got(kind, b):
        return land[kind * blocks + b].astype(F32)

    def local(slot, b):
        return sums[slot * blocks + b].astype(F32)

    def share(i):
        who = rep_others[i]
        return remote(wsend.at[who], a0.at[me.rep], e0s.at[i], e0r.at[i], me.at_rep(who))

    def along_x(i):
        who = x_others[i]
        return remote(a0.at[who], a1.at[i], e1s.at[i], e1r.at[i], me.at_x(who))

    def scatter_rows(d):
        who = lax.rem(me.row + d, rows)
        return remote(piece.at[who], a2.at[d], e2s.at[d], e2r.at[d], me.at_row(who))

    def gather_rows(d):
        who = lax.rem(me.row + d, rows)
        return remote(done, a3.at[me.row], e3s.at[d], e3r.at[d], me.at_row(who))

    def gather_x(i):
        return remote(a3, a4.at[me.x], e4s.at[i], e4r.at[i], me.at_x(x_others[i]))

    for p in range(4):
        wsend[p] = wgrad[p].astype(BF)
    for i in range(3):
        share(i).start()
    a0[me.rep] = wsend[me.rep]

    @pl.loop(0, nc)
    def _(c):
        halo(POST, c).start()
        halo(DIAG, c).start()
        halo(Q, c).start()

    @pl.loop(0, nc + 6)
    def _(s):
        @pl.when(s < nc)
        def _():
            c = s
            halo(POST, c).wait_recv()
            for i in range(hb):
                b = c * hb + i
                out[b] = (local(me.slot_p, b) + got(POST, b)).astype(BF)
            halo(PP, c).start()

        @pl.when((s >= 2) & (s < nc + 2))
        def _():
            c = s - 2
            halo(DIAG, c).wait_recv()
            halo(Q, c).wait_recv()
            for i in range(hb):
                b = c * hb + i
                out[blocks + b] = (local(me.slot_n2, b) + got(DIAG, b) + got(Q, b)).astype(BF)
            halo(N2, c).start()

        @pl.when((s >= 3) & (s < nc + 3))
        def _():
            c = s - 3
            halo(PP, c).wait_recv()
            for i in range(hb):
                b = c * hb + i
                out[2 * blocks + b] = (local(me.slot_n1, b) + got(PP, b)).astype(BF)
            halo(N1, c).start()

        @pl.when(s == 2)
        def _():
            for i in range(3):
                share(i).wait_recv()
            for i in range(3):
                along_x(i).start()

        @pl.when(s == 6)
        def _():
            for i in range(3):
                along_x(i).wait_recv()
            total = a0[me.x].astype(F32)
            for i in range(3):
                total += a1[i].astype(F32)
            piece[...] = total.reshape(piece.shape)
            for d in range(1, rows):
                scatter_rows(d).start()

        @pl.when(s == 8)
        def _():
            for d in range(1, rows):
                scatter_rows(d).wait_recv()
            total = piece[me.row]
            for d in range(1, rows):
                total += a2[d]
            done[...] = total
            a3[me.row] = total
            for d in range(1, rows):
                gather_rows(d).start()

        @pl.when(s == 10)
        def _():
            for d in range(1, rows):
                gather_rows(d).wait_recv()
            for i in range(3):
                gather_x(i).start()
            a4[me.x] = a3[...]

        @pl.when(s >= 6)
        def _():
            c = s - 6
            halo(N2, c).wait_recv()
            halo(N1, c).wait_recv()
            for i in range(hb):
                b = c * hb + i
                total = own_sums[b] + back_root[b] + got(N1, b) + got(N2, b)
                grad_feat[b] = lax.dot_general(
                    onehot(order, b), total.astype(BF), NT, preferred_element_type=F32
                ).astype(BF)

    for i in range(3):
        gather_x(i).wait_recv()
    for p in range(4):
        both = a4[p].reshape(2 * width, width)
        grad_rel[p * width : (p + 1) * width, :] = both[:width]
        grad_root[p * width : (p + 1) * width, :] = both[width:]

    @pl.loop(0, nc)
    def _(c):
        for kind in range(6):
            halo(kind, c).wait_send()

    for i in range(3):
        share(i).wait_send()
        along_x(i).wait_send()
        gather_x(i).wait_send()
    for d in range(1, rows):
        scatter_rows(d).wait_send()
        gather_rows(d).wait_send()


def on_device(features, order, columns, tiles, w_rel, w_root, upstream):
    groups = lax.axis_size("blk")
    blocks, bl = order.shape
    width = features.shape[1]
    rows = groups // ROW
    vmem = pl.BlockSpec(memory_space=pltpu.VMEM)
    smem = pl.BlockSpec(memory_space=pltpu.SMEM)
    anywhere = pl.BlockSpec(memory_space=pl.ANY)
    dma = pltpu.SemaphoreType.DMA
    cube = (blocks, bl, width)
    mrows = blocks // MID_CHUNKS * bl

    def shape(dims, dtype):
        return jax.ShapeDtypeStruct(dims, dtype)

    hidden, back_agg, back_root, wgrad = pl.pallas_call(
        lambda *refs: forward_kernel(groups, *refs),
        out_shape=(
            shape(cube, BF),
            shape((blocks, width, bl), BF),
            shape((blocks, width, bl), F32),
            shape((4, 2 * width, width), F32),
        ),
        in_specs=[smem, vmem, vmem, anywhere, vmem, vmem, vmem],
        out_specs=(vmem,) * 4,
        scratch_shapes=[
            pltpu.VMEM((SPAN * blocks, bl, width), BF),
            pltpu.VMEM(tiles.shape, BF),
            pltpu.VMEM(cube, BF),
            pltpu.VMEM((4, 2 * width, width), BF),
            pltpu.VMEM((MID_CHUNKS, 2, mrows, width), F32),
            pltpu.VMEM((MID_CHUNKS, 2, mrows, width), BF),
            pltpu.VMEM((MID_CHUNKS, 2, mrows, width), BF),
            pltpu.VMEM((MID_CHUNKS, mrows, width), BF),
            pltpu.VMEM((MID_CHUNKS, mrows, width), BF),
            pltpu.VMEM((4,) + cube, BF),
            dma(()),
            dma((6, HALO_CHUNKS)),
            dma((6, HALO_CHUNKS)),
            dma((3, 2)),
            dma((3, 2)),
            dma((5, MID_CHUNKS)),
            dma((5, MID_CHUNKS)),
        ],
        compiler_params=pltpu.CompilerParams(
            collective_id=0, has_side_effects=True, vmem_limit_bytes=56 * MIB
        ),
        name="forward",
    )(columns, features.reshape(cube), order, tiles, w_rel, w_root, upstream.reshape(cube))

    sums, own_sums = pl.pallas_call(
        lambda *refs: push_kernel(groups, *refs),
        grid=(blocks,),
        out_shape=(shape((SPAN * blocks, width, bl), BF), shape((blocks, width, bl), F32)),
        in_specs=[
            smem,
            pl.BlockSpec((1,) + tiles.shape[1:], lambda i: (i, 0, 0, 0)),
            pl.BlockSpec((1, width, bl), lambda i: (i, 0, 0)),
        ],
        out_specs=(
            pl.BlockSpec((SPAN * blocks, width, bl), lambda i: (0, 0, 0)),
            pl.BlockSpec((blocks, width, bl), lambda i: (0, 0, 0)),
        ),
        scratch_shapes=[pltpu.VMEM((SPAN * blocks, width, bl), F32)],
        compiler_params=pltpu.CompilerParams(vmem_limit_bytes=48 * MIB),
        name="push",
    )(columns, tiles, back_agg)

    piece = (2 * width // rows, width)
    grad_feat, grad_rel, grad_root = pl.pallas_call(
        lambda *refs: backward_kernel(groups, *refs),
        out_shape=(
            shape(cube, BF),
            shape((4 * width, width), F32),
            shape((4 * width, width), F32),
        ),
        in_specs=[vmem] * 5,
        out_specs=(vmem,) * 3,
        scratch_shapes=[
            pltpu.VMEM((6 * blocks, width, bl), BF),
            pltpu.VMEM((3 * blocks, width, bl), BF),
            pltpu.VMEM((4, 2 * width, width), BF),
            pltpu.VMEM((4, 2 * width, width), BF),
            pltpu.VMEM((3, 2 * width, width), BF),
            pltpu.VMEM((rows,) + piece, F32),
            pltpu.VMEM((rows,) + piece, F32),
            pltpu.VMEM((4, rows) + piece, F32),
            pltpu.VMEM((rows,) + piece, F32),
            pltpu.VMEM(piece, F32),
            dma((6, BACK_CHUNKS)),
            dma((6, BACK_CHUNKS)),
            dma((3,)), dma((3,)),
            dma((3,)), dma((3,)),
            dma((rows,)), dma((rows,)),
            dma((rows,)), dma((rows,)),
            dma((3,)), dma((3,)),
        ],
        compiler_params=pltpu.CompilerParams(
            collective_id=1, has_side_effects=True, vmem_limit_bytes=48 * MIB
        ),
        name="backward",
    )(sums, own_sums, back_root, order, wgrad)

    flat = (blocks * bl, width)
    return hidden.reshape(flat), grad_feat.reshape(flat), grad_rel, grad_root


def solution(mesh):
    in_specs = (
        P("blk", "rep"),
        P("blk", None),
        P("blk", None),
        P("blk", None, None, None),
        P(None, "rep"),
        P(None, "rep"),
        P("blk", "rep"),
    )
    out_specs = (P("blk", "rep"), P("blk", "rep"), P(None, "rep"), P(None, "rep"))
    return jax.shard_map(
        on_device, mesh=mesh, in_specs=in_specs, out_specs=out_specs, check_vma=False
    )
```

```python
import jax
import jax.numpy as jnp
from jax import lax
from jax.experimental import pallas as pl
from jax.experimental.pallas import tpu as pltpu
from jax.sharding import PartitionSpec as P

MESH = pl.DeviceIdType.MESH
REACH = 3
SPAN = 2 * REACH + 1
ROW = 4
HALO_CHUNKS = 8
MID_CHUNKS = 8
BACK_CHUNKS = 8
BF = jnp.bfloat16
F32 = jnp.float32
NT = (((1,), (1,)), ((), ()))
TN = (((0,), (0,)), ((), ()))
MIB = 2**20


class Place:
    def __init__(self, groups):
        blk = lax.axis_index("blk")
        rep = lax.axis_index("rep")
        self.groups = groups
        self.rows = groups // ROW
        self.blk, self.rep = blk, rep
        x = lax.rem(blk, ROW)
        self.x = x
        self.row = lax.div(blk, ROW)
        half, odd = lax.div(x, 2), lax.rem(x, 2)
        self.n1 = 3 - x
        self.n2 = x + 1 - 2 * odd
        self.diag = lax.rem(x + 2, 4)
        self.step_p = 1 - 2 * half
        self.step_q = 1 - 2 * odd
        self.slot_n1 = REACH + self.n1 - x
        self.slot_n2 = REACH + self.n2 - x
        self.slot_diag = REACH + self.diag - x
        self.slot_p = REACH + self.n1 - x - ROW * self.step_p
        self.slot_q = REACH + self.n2 - x - ROW * self.step_q
        self.slot_post = 1 + 4 * half
        self.core = lax.rem(rep, 2)
        self.low = lax.div(rep, 2)
        self.rep_sib = 2 * self.low + 1 - self.core
        self.rep_y = 2 * (1 - self.low) + self.core
        self.rep_far = 2 * (1 - self.low) + 1 - self.core

    def at_x(self, x):
        return (self.row * ROW + x, self.rep)

    def at_row(self, row):
        return (row * ROW + self.x, self.rep)

    def row_by(self, step):
        return self.at_row(lax.rem(self.row + step + self.rows, self.rows))

    def near(self, d):
        at = lax.rem(self.x * 4 + self.rep + d, 16)
        return (self.row * ROW + lax.div(at, 4), lax.rem(at, 4))

    def at_rep(self, rep):
        return (self.blk, rep)


def greet(partners):
    barrier = pltpu.get_barrier_semaphore()
    for who in partners:
        pl.semaphore_signal(barrier, inc=1, device_id=who, device_id_type=MESH)
    pl.semaphore_wait(barrier, len(partners))


def remote(src, dst, send, recv, who):
    return pltpu.make_async_remote_copy(
        src_ref=src, dst_ref=dst, send_sem=send, recv_sem=recv, device_id=who, device_id_type=MESH
    )


def onehot(order_ref, b):
    length = order_ref.shape[1]
    node = lax.broadcasted_iota(jnp.int32, (length, length), 0)
    return (node == order_ref[pl.ds(b, 1), :]).astype(F32).astype(BF)


def slot_of(col, place, blocks):
    group = lax.shift_right_arithmetic(col, jnp.int32(blocks.bit_length() - 1))
    offset = (group - place.blk + REACH + place.groups) & (place.groups - 1)
    return jnp.minimum(offset, SPAN - 1) * blocks + (col & (blocks - 1))


def sort_entries(cols_row, place, blocks, meta):
    count = cols_row.shape[1]
    slot = slot_of(cols_row, place, blocks)
    entry = lax.broadcasted_iota(jnp.int32, (count, count), 1)
    slots = jnp.broadcast_to(slot, (count, count))
    slots_t = slots.T
    keys, keys_t = slots * count + entry, slots_t * count + entry.T
    earlier = (keys_t < keys).astype(jnp.int32)
    rank = jnp.sum(earlier, axis=0, keepdims=True)
    same = jnp.sum(jnp.where(slots_t == slots, earlier, 0), axis=0, keepdims=True)
    rank_t = jnp.broadcast_to(rank, (count, count)).T
    same_t = jnp.broadcast_to(same, (count, count)).T
    here = rank_t == entry
    meta[0:1, :] = jnp.sum(jnp.where(here, entry.T, 0), axis=0, keepdims=True)
    meta[1:2, :] = jnp.sum(jnp.where(here, jnp.minimum(same_t, 1), 0), axis=0, keepdims=True)
    upto = jnp.sum((slots_t <= entry).astype(jnp.int32), axis=0, keepdims=True)
    meta[2:3, :] = jnp.maximum(upto - 1, 0)
    found = jnp.sum((slots_t == entry).astype(jnp.int32), axis=0, keepdims=True)
    meta[3:4, :] = jnp.minimum(found, 1)


def layer_kernel(
    groups,
    cols, feat, order, tiles, w_rel, w_root, upstream,
    hidden, grad_feat, grad_rel, grad_root,
    win, tbuf, agg, slab, keep, s1, r1, s2, r2, pre, back_root, wgrad, prod, meta, meta_s,
    land, wsend, a1, a2, a3, a4, piece, done,
    tile_sem, meta_sem, hs, hr, ws, wr, ms, mr,
    bs, br, e0s, e0r, e2s, e2r, e3s, e3r, e4s, e4r,
):
    me = Place(groups)
    blocks, bl, width = feat.shape
    per_row = cols.shape[1]
    entries = blocks * per_row
    own = REACH * blocks
    nc = HALO_CHUNKS
    hb = blocks // nc
    nm = MID_CHUNKS
    mb = blocks // nm
    mrows = mb * bl

    tile_copy = pltpu.make_async_copy(tiles, tbuf, tile_sem)
    tile_copy.start()
    sib, far_y = me.at_rep(me.rep_sib), me.at_rep(me.rep_y)
    greet([me.near(d) for d in range(1, 16)] + [me.row_by(d) for d in range(1, me.rows)])

    def halo(kind, c):
        src_slot, dst_slot, who = [
            (REACH, REACH + me.x - me.n1, me.at_x(me.n1)),
            (REACH, REACH + me.x - me.n2, me.at_x(me.n2)),
            (me.slot_n2, REACH + me.n2 - me.n1, me.at_x(me.n1)),
            (me.slot_n1, me.slot_p, me.row_by(me.step_p)),
            (me.slot_n2, me.slot_q, me.row_by(me.step_q)),
            (me.slot_p, me.slot_post, me.at_x(me.n2)),
        ][kind]
        return remote(
            win.at[pl.ds(src_slot * blocks + c * hb, hb)],
            win.at[pl.ds(dst_slot * blocks + c * hb, hb)],
            hs.at[kind, c], hr.at[kind, c], who,
        )

    @pl.loop(0, nc)
    def _(c):
        for i in range(hb):
            b = c * hb + i
            win[own + b] = lax.dot_general(
                onehot(order, b), feat[b], TN, preferred_element_type=F32
            ).astype(BF)
        halo(0, c).start()
        halo(1, c).start()

    def weight(i, j):
        who = (me.rep_sib, me.rep_y, me.rep_far)[i]
        src = (w_rel, w_root)[j]
        return remote(
            src.at[pl.ds(who * width, width)], slab.at[me.rep, pl.ds(j * width, width)],
            ws.at[i, j], wr.at[i, j], me.at_rep(who),
        )

    for i in range(3):
        for j in range(2):
            weight(i, j).start()
    for j, src in enumerate((w_rel, w_root)):
        slab[me.rep, j * width : (j + 1) * width] = src[pl.ds(me.rep * width, width), :]

    place_of = lax.broadcasted_iota(jnp.int32, (1, entries), 1)

    def collect(b, row):
        for k in range(per_row):
            row = jnp.where(place_of == b * per_row + k, cols[b, k], row)
        return row

    cols_row = lax.fori_loop(0, blocks, collect, jnp.zeros((1, entries), jnp.int32))
    sort_entries(cols_row, me, blocks, meta)
    meta_copy = pltpu.make_async_copy(meta, meta_s, meta_sem)
    meta_copy.start()

    @pl.loop(0, nc + 2)
    def _(s):
        @pl.when(s < nc)
        def _():
            halo(0, s).wait_recv()
            halo(1, s).wait_recv()
            halo(2, s).start()
            halo(3, s).start()
            halo(4, s).start()

        @pl.when(s >= 2)
        def _():
            halo(3, s - 2).wait_recv()
            halo(5, s - 2).start()

    @pl.loop(0, nc)
    def _(c):
        for kind in (2, 4, 5):
            halo(kind, c).wait_recv()

    for i in range(3):
        for j in range(2):
            weight(i, j).wait_recv()
    tile_copy.wait()
    meta_copy.wait()

    panel_sib = [2 * (1 - me.low) + 1 - me.core, 2 * me.low + 1 - me.core]
    panel_mine = [me.rep_y, me.rep]

    def rows(c):
        return pl.ds(c * mb, mb)

    def mid(kind, c):
        src, dst, who = [
            (s1.at[c], r1.at[c], sib),
            (s2.at[c], r2.at[c], far_y),
            (pre.at[me.rep, rows(c)], pre.at[me.rep, rows(c)], far_y),
            (pre.at[me.rep, rows(c)], pre.at[me.rep, rows(c)], sib),
            (pre.at[me.rep_y, rows(c)], pre.at[me.rep_y, rows(c)], sib),
        ][kind]
        return remote(src, dst, ms.at[kind, c], mr.at[kind, c], who)

    def both(c):
        return jnp.concatenate(
            [
                agg[rows(c)].reshape(mrows, width),
                win[pl.ds(own + c * mb, mb)].reshape(mrows, width),
            ],
            axis=1,
        )

    @pl.loop(0, nm + 4)
    def _(s):
        @pl.when(s < nm)
        def _():
            for i in range(mb):
                b = s * mb + i
                left = jnp.concatenate([tbuf[b, k] for k in range(per_row)], axis=1)
                right = jnp.concatenate(
                    [win[slot_of(cols[b, k], me, blocks)] for k in range(per_row)], axis=0
                )
                agg[b] = jnp.dot(left, right, preferred_element_type=F32).astype(BF)
            x = both(s)
            for i in range(2):
                part = jnp.dot(x, slab[panel_sib[i]], preferred_element_type=F32)
                s1[s, i] = part.astype(BF)
            mid(0, s).start()
            for i in range(2):
                keep[s, i] = jnp.dot(x, slab[panel_mine[i]], preferred_element_type=F32)

        @pl.when((s >= 1) & (s < nm + 1))
        def _():
            c = s - 1
            mid(0, c).wait_recv()
            s2[c] = (keep[c, 0] + r1[c, 0].astype(F32)).astype(BF)
            mid(1, c).start()

        @pl.when((s >= 2) & (s < nm + 2))
        def _():
            c = s - 2
            mid(1, c).wait_recv()
            v = keep[c, 1] + r1[c, 1].astype(F32) + r2[c].astype(F32)
            sq = v * v
            t = jnp.tanh(0.7978845608 * (v + 0.044715 * (sq * v)))
            up = upstream[rows(c)].reshape(mrows, width).astype(F32)
            hidden[rows(c)] = (0.5 * v * (1.0 + t)).astype(BF).reshape(mb, bl, width)
            slope = 0.5 * (1.0 + t) + 0.5 * v * (1.0 - t * t) * (
                0.7978845608 * (1.0 + 0.134145 * sq)
            )
            pre[me.rep, rows(c)] = (up * slope).astype(BF).reshape(mb, bl, width)
            mid(2, c).start()
            mid(3, c).start()

        @pl.when((s >= 3) & (s < nm + 3))
        def _():
            mid(2, s - 3).wait_recv()
            mid(4, s - 3).start()

        @pl.when(s >= 4)
        def _():
            c = s - 4
            mid(3, c).wait_recv()
            mid(4, c).wait_recv()
            x = both(c)
            gathered = jnp.concatenate(
                [pre[p, rows(c)].reshape(mrows, width) for p in range(4)], axis=1
            )
            slabs = jnp.concatenate([slab[p] for p in range(4)], axis=1)
            back = lax.dot_general(slabs, gathered, NT, preferred_element_type=F32)
            for i in range(mb):
                cut = back[:, i * bl : (i + 1) * bl]
                b = c * mb + i
                back_root[b] = cut[width:]
                right = jnp.concatenate([tbuf[b, k] for k in range(per_row)], axis=1)
                res = jnp.dot(cut[:width].astype(BF), right, preferred_element_type=F32)
                for k in range(per_row):
                    prod[b * per_row + k] = res[:, k * bl : (k + 1) * bl]
            grads = lax.dot_general(x, gathered, TN, preferred_element_type=F32)

            @pl.when(c == 0)
            def _():
                for p in range(4):
                    wgrad[p] = grads[:, p * width : (p + 1) * width]

            @pl.when(c > 0)
            def _():
                for p in range(4):
                    wgrad[p] += grads[:, p * width : (p + 1) * width]

    na = BACK_CHUNKS
    ab = blocks // na
    rows_all = me.rows
    x_others = [me.n1, me.n2, me.diag]
    POST, DIAG, Q, PP, N2, N1 = range(6)

    def part(ref, slot, c):
        return ref.at[pl.ds(slot * blocks + c * ab, ab)]

    out = win
    @pl.loop(0, nc)
    def _(c):
        for kind in range(6):
            halo(kind, c).wait_send()

    def back(kind, c):
        _, who = [
            (POST, me.at_x(me.n2)),
            (DIAG, me.at_x(me.n1)),
            (Q, me.row_by(-me.step_q)),
            (PP, me.row_by(-me.step_p)),
            (N2, me.at_x(me.n2)),
            (N1, me.at_x(me.n1)),
        ][kind]
        return remote(part(out, kind, c), part(land, kind, c), bs.at[kind, c], br.at[kind, c], who)

    def got(kind, b):
        return land[kind * blocks + b].astype(F32)

    def local(slot, b):
        at = slot * blocks + b
        last = meta_s[2, at]
        return tbuf[lax.div(last, per_row), lax.rem(last, per_row)].astype(F32) * meta_s[3, at].astype(F32)

    alone = me.x == me.rep

    def give(p):
        return remote(
            wsend.at[p], a1.at[me.x], e0s.at[p], e0r.at[me.x], (me.row * ROW + me.rep, p)
        )

    def take(x):
        return remote(wsend.at[0], a1.at[x], e0s.at[0], e0r.at[x], (me.row * ROW + x, me.x))

    def unless_self(i, mine, act):
        @pl.when(jnp.logical_not(alone & (mine == i)))
        def _():
            act(i)

    def scatter_rows(d):
        who = lax.rem(me.row + d, rows_all)
        return remote(piece.at[who], a2.at[d], e2s.at[d], e2r.at[d], me.at_row(who))

    def gather_rows(d):
        who = lax.rem(me.row + d, rows_all)
        return remote(done, a3.at[me.row], e3s.at[d], e3r.at[d], me.at_row(who))

    def gather_x(i):
        return remote(a3, a4.at[me.x], e4s.at[i], e4r.at[i], me.at_x(x_others[i]))

    for p in range(4):
        wsend[p] = wgrad[p].astype(BF)
    for p in range(4):
        unless_self(p, me.rep, lambda i: give(i).start())

    @pl.when(alone)
    def _():
        a1[me.x] = wsend[me.rep]

    def add(e, total):
        total = total * meta_s[1, e].astype(F32) + prod[meta_s[0, e]]
        tbuf[lax.div(e, per_row), lax.rem(e, per_row)] = total.astype(BF)
        return total

    lax.fori_loop(0, entries, add, jnp.zeros((width, bl), F32), unroll=4)
    for x in range(4):
        unless_self(x, me.x, lambda i: take(i).wait_recv())
    summed = a1[0].astype(F32)
    for x in range(1, 4):
        summed += a1[x].astype(F32)
    piece[...] = summed.reshape(piece.shape)
    for d in range(1, rows_all):
        scatter_rows(d).start()

    @pl.loop(0, na + 6)
    def _(s):
        @pl.when(s < na)
        def _():
            c = s
            for kind, slot in ((POST, me.slot_post), (DIAG, me.slot_diag), (Q, me.slot_q)):
                for i in range(ab):
                    b = c * ab + i
                    out[kind * blocks + b] = local(slot, b).astype(BF)
                back(kind, c).start()

        @pl.when((s >= 2) & (s < na + 2))
        def _():
            c = s - 2
            back(POST, c).wait_recv()
            for i in range(ab):
                b = c * ab + i
                out[PP * blocks + b] = (local(me.slot_p, b) + got(POST, b)).astype(BF)
            back(PP, c).start()

        @pl.when((s >= 4) & (s < na + 4))
        def _():
            c = s - 4
            back(DIAG, c).wait_recv()
            back(Q, c).wait_recv()
            for i in range(ab):
                b = c * ab + i
                out[N2 * blocks + b] = (local(me.slot_n2, b) + got(DIAG, b) + got(Q, b)).astype(BF)
            back(N2, c).start()

        @pl.when((s >= 4) & (s < na + 4))
        def _():
            c = s - 4
            back(PP, c).wait_recv()
            for i in range(ab):
                b = c * ab + i
                out[N1 * blocks + b] = (local(me.slot_n1, b) + got(PP, b)).astype(BF)
            back(N1, c).start()

        @pl.when(s == 3)
        def _():
            for d in range(1, rows_all):
                scatter_rows(d).wait_recv()
            total = piece[me.row]
            for d in range(1, rows_all):
                total += a2[d]
            done[...] = total.astype(BF)
            a3[me.row] = total.astype(BF)
            for d in range(1, rows_all):
                gather_rows(d).start()

        @pl.when(s == 7)
        def _():
            for d in range(1, rows_all):
                gather_rows(d).wait_recv()
            for i in range(3):
                gather_x(i).start()
            a4[me.x] = a3[...]

        @pl.when(s >= 6)
        def _():
            c = s - 6
            back(N2, c).wait_recv()
            back(N1, c).wait_recv()
            for i in range(ab):
                b = c * ab + i
                total = local(REACH, b) + back_root[b] + got(N1, b) + got(N2, b)
                grad_feat[b] = lax.dot_general(
                    onehot(order, b), total.astype(BF), NT, preferred_element_type=F32
                ).astype(BF)

    for i in range(3):
        gather_x(i).wait_recv()
    for p in range(4):
        both = a4[p].reshape(2 * width, width).astype(F32)
        grad_rel[p * width : (p + 1) * width, :] = both[:width]
        grad_root[p * width : (p + 1) * width, :] = both[width:]

    @pl.loop(0, na)
    def _(c):
        for kind in range(6):
            back(kind, c).wait_send()

    for i in range(3):
        gather_x(i).wait_send()
    for p in range(4):
        unless_self(p, me.rep, lambda i: give(i).wait_send())
    for d in range(1, rows_all):
        scatter_rows(d).wait_send()
        gather_rows(d).wait_send()

    @pl.loop(0, nm)
    def _(c):
        for kind in range(5):
            mid(kind, c).wait_send()

    for i in range(3):
        for j in range(2):
            weight(i, j).wait_send()


def on_device(features, order, columns, tiles, w_rel, w_root, upstream):
    groups = lax.axis_size("blk")
    blocks, bl = order.shape
    width = features.shape[1]
    rows = groups // ROW
    vmem = pl.BlockSpec(memory_space=pltpu.VMEM)
    smem = pl.BlockSpec(memory_space=pltpu.SMEM)
    anywhere = pl.BlockSpec(memory_space=pl.ANY)
    dma = pltpu.SemaphoreType.DMA
    cube = (blocks, bl, width)
    mrows = blocks // MID_CHUNKS * bl

    def shape(dims, dtype):
        return jax.ShapeDtypeStruct(dims, dtype)

    piece = (2 * width // rows, width)
    entries = columns.size
    hidden, grad_feat, grad_rel, grad_root = pl.pallas_call(
        lambda *refs: layer_kernel(groups, *refs),
        out_shape=(
            shape(cube, BF),
            shape(cube, BF),
            shape((4 * width, width), F32),
            shape((4 * width, width), F32),
        ),
        in_specs=[smem, vmem, vmem, anywhere, vmem, vmem, vmem],
        out_specs=(vmem,) * 4,
        scratch_shapes=[
            pltpu.VMEM((SPAN * blocks, bl, width), BF),
            pltpu.VMEM(tiles.shape, BF),
            pltpu.VMEM(cube, BF),
            pltpu.VMEM((4, 2 * width, width), BF),
            pltpu.VMEM((MID_CHUNKS, 2, mrows, width), F32),
            pltpu.VMEM((MID_CHUNKS, 2, mrows, width), BF),
            pltpu.VMEM((MID_CHUNKS, 2, mrows, width), BF),
            pltpu.VMEM((MID_CHUNKS, mrows, width), BF),
            pltpu.VMEM((MID_CHUNKS, mrows, width), BF),
            pltpu.VMEM((4,) + cube, BF),
            pltpu.VMEM((blocks, width, bl), F32),
            pltpu.VMEM((4, 2 * width, width), F32),
            pltpu.VMEM((entries, width, bl), F32),
            pltpu.VMEM((8, entries), jnp.int32),
            pltpu.SMEM((8, entries), jnp.int32),
            pltpu.VMEM((6 * blocks, width, bl), BF),
            pltpu.VMEM((4, 2 * width, width), BF),
            pltpu.VMEM((4, 2 * width, width), BF),
            pltpu.VMEM((rows,) + piece, F32),
            pltpu.VMEM((rows,) + piece, BF),
            pltpu.VMEM((4, rows) + piece, BF),
            pltpu.VMEM((rows,) + piece, F32),
            pltpu.VMEM(piece, BF),
            dma(()),
            dma(()),
            dma((6, HALO_CHUNKS)),
            dma((6, HALO_CHUNKS)),
            dma((3, 2)),
            dma((3, 2)),
            dma((5, MID_CHUNKS)),
            dma((5, MID_CHUNKS)),
            dma((6, BACK_CHUNKS)),
            dma((6, BACK_CHUNKS)),
            dma((4,)), dma((4,)),
            dma((rows,)), dma((rows,)),
            dma((rows,)), dma((rows,)),
            dma((3,)), dma((3,)),
        ],
        compiler_params=pltpu.CompilerParams(
            collective_id=0, has_side_effects=True, vmem_limit_bytes=46 * MIB
        ),
        name="layer",
    )(
        columns, features.reshape(cube), order, tiles, w_rel, w_root,
        upstream.reshape(cube),
    )

    flat = (blocks * bl, width)
    return hidden.reshape(flat), grad_feat.reshape(flat), grad_rel, grad_root


def solution(mesh):
    in_specs = (
        P("blk", "rep"),
        P("blk", None),
        P("blk", None),
        P("blk", None, None, None),
        P(None, "rep"),
        P(None, "rep"),
        P("blk", "rep"),
    )
    out_specs = (P("blk", "rep"), P("blk", "rep"), P(None, "rep"), P(None, "rep"))
    return jax.shard_map(
        on_device, mesh=mesh, in_specs=in_specs, out_specs=out_specs, check_vma=False
    )
```

```python
import jax
import jax.numpy as jnp
from jax import lax
from jax.experimental import pallas as pl
from jax.experimental.pallas import tpu as pltpu
from jax.sharding import PartitionSpec as P

MESH = pl.DeviceIdType.MESH
REACH = 3
SPAN = 2 * REACH + 1
ROW = 4
HALO_CHUNKS = 4
MID_CHUNKS = 8
BACK_CHUNKS = 16
MID_LAGS = (1, 3, 5, 6)
BACK_LAGS = (2, 5, 8)
WGRAD_STEPS = (5, 11, 17)
BF = jnp.bfloat16
F32 = jnp.float32
NT = (((1,), (1,)), ((), ()))
TN = (((0,), (0,)), ((), ()))
MIB = 2**20


class Place:
    def __init__(self, groups):
        blk = lax.axis_index("blk")
        rep = lax.axis_index("rep")
        self.groups = groups
        self.rows = groups // ROW
        self.blk, self.rep = blk, rep
        x = lax.rem(blk, ROW)
        self.x = x
        self.row = lax.div(blk, ROW)
        half, odd = lax.div(x, 2), lax.rem(x, 2)
        self.n1 = 3 - x
        self.n2 = x + 1 - 2 * odd
        self.diag = lax.rem(x + 2, 4)
        self.step_p = 1 - 2 * half
        self.step_q = 1 - 2 * odd
        self.slot_n1 = REACH + self.n1 - x
        self.slot_n2 = REACH + self.n2 - x
        self.slot_diag = REACH + self.diag - x
        self.slot_p = REACH + self.n1 - x - ROW * self.step_p
        self.slot_q = REACH + self.n2 - x - ROW * self.step_q
        self.slot_post = 1 + 4 * half
        self.core = lax.rem(rep, 2)
        self.low = lax.div(rep, 2)
        self.rep_sib = 2 * self.low + 1 - self.core
        self.rep_y = 2 * (1 - self.low) + self.core
        self.rep_far = 2 * (1 - self.low) + 1 - self.core

    def at_x(self, x):
        return (self.row * ROW + x, self.rep)

    def at_row(self, row):
        return (row * ROW + self.x, self.rep)

    def row_by(self, step):
        return self.at_row(lax.rem(self.row + step + self.rows, self.rows))

    def near(self, d):
        at = lax.rem(self.x * 4 + self.rep + d, 16)
        return (self.row * ROW + lax.div(at, 4), lax.rem(at, 4))

    def at_rep(self, rep):
        return (self.blk, rep)


def greet(partners):
    barrier = pltpu.get_barrier_semaphore()
    for who in partners:
        pl.semaphore_signal(barrier, inc=1, device_id=who, device_id_type=MESH)
    pl.semaphore_wait(barrier, len(partners))


def remote(src, dst, send, recv, who):
    return pltpu.make_async_remote_copy(
        src_ref=src, dst_ref=dst, send_sem=send, recv_sem=recv, device_id=who, device_id_type=MESH
    )


def onehot(order_ref, b):
    length = order_ref.shape[1]
    node = lax.broadcasted_iota(jnp.int32, (length, length), 0)
    return (node == order_ref[pl.ds(b, 1), :]).astype(F32).astype(BF)


def slot_of(col, place, blocks):
    group = lax.shift_right_arithmetic(col, jnp.int32(blocks.bit_length() - 1))
    offset = (group - place.blk + REACH + place.groups) & (place.groups - 1)
    return jnp.minimum(offset, SPAN - 1) * blocks + (col & (blocks - 1))


def sort_entries(cols_row, place, blocks, meta):
    count = cols_row.shape[1]
    slot = slot_of(cols_row, place, blocks)
    entry = lax.broadcasted_iota(jnp.int32, (count, count), 1)
    slots = jnp.broadcast_to(slot, (count, count))
    slots_t = slots.T
    keys, keys_t = slots * count + entry, slots_t * count + entry.T
    earlier = (keys_t < keys).astype(jnp.int32)
    rank = jnp.sum(earlier, axis=0, keepdims=True)
    same = jnp.sum(jnp.where(slots_t == slots, earlier, 0), axis=0, keepdims=True)
    rank_t = jnp.broadcast_to(rank, (count, count)).T
    same_t = jnp.broadcast_to(same, (count, count)).T
    here = rank_t == entry
    meta[0:1, :] = jnp.sum(jnp.where(here, entry.T, 0), axis=0, keepdims=True)
    meta[1:2, :] = jnp.sum(jnp.where(here, jnp.minimum(same_t, 1), 0), axis=0, keepdims=True)
    upto = jnp.sum((slots_t <= entry).astype(jnp.int32), axis=0, keepdims=True)
    meta[2:3, :] = jnp.maximum(upto - 1, 0)
    found = jnp.sum((slots_t == entry).astype(jnp.int32), axis=0, keepdims=True)
    meta[3:4, :] = jnp.minimum(found, 1)


def layer_kernel(
    groups,
    cols_in, feat_in, order_in, tiles, w_rel_in, w_root_in, upstream_in,
    hidden, grad_feat, grad_rel, grad_root,
    cols, feat, order, w_rel, w_root, upstream, win, tbuf, agg, slab, keep, s1, r1, s2, r2, pre, back_root, wgrad, prod, meta, meta_s,
    land, wsend, a1, a2, a3, a4, piece, done,
    in_sem, tile_sem, meta_sem, hs, hr, ws, wr, ms, mr,
    bs, br, e0s, e0r, e2s, e2r, e3s, e3r, e4s, e4r,
):
    me = Place(groups)
    blocks, bl, width = feat.shape
    per_row = cols.shape[1]
    entries = blocks * per_row
    own = REACH * blocks
    nc = HALO_CHUNKS
    hb = blocks // nc
    nm = MID_CHUNKS
    mb = blocks // nm
    mrows = mb * bl

    loads = [
        pltpu.make_async_copy(src, dst, in_sem.at[i])
        for i, (src, dst) in enumerate(
            (
                (feat_in, feat),
                (order_in, order),
                (w_rel_in, w_rel),
                (w_root_in, w_root),
                (cols_in, cols),
                (upstream_in, upstream),
            )
        )
    ]
    for load in loads:
        load.start()
    tile_copy = pltpu.make_async_copy(tiles, tbuf, tile_sem)
    tile_copy.start()
    sib, far_y = me.at_rep(me.rep_sib), me.at_rep(me.rep_y)
    greet([me.near(d) for d in range(1, 16)] + [me.row_by(d) for d in range(1, me.rows)])

    loads[0].wait()
    loads[1].wait()

    def halo(kind, c):
        src_slot, dst_slot, who = [
            (REACH, REACH + me.x - me.n1, me.at_x(me.n1)),
            (REACH, REACH + me.x - me.n2, me.at_x(me.n2)),
            (me.slot_n2, REACH + me.n2 - me.n1, me.at_x(me.n1)),
            (me.slot_n1, me.slot_p, me.row_by(me.step_p)),
            (me.slot_n2, me.slot_q, me.row_by(me.step_q)),
            (me.slot_p, me.slot_post, me.at_x(me.n2)),
        ][kind]
        return remote(
            win.at[pl.ds(src_slot * blocks + c * hb, hb)],
            win.at[pl.ds(dst_slot * blocks + c * hb, hb)],
            hs.at[kind, c], hr.at[kind, c], who,
        )

    @pl.loop(0, nc)
    def _(c):
        for i in range(hb):
            b = c * hb + i
            win[own + b] = lax.dot_general(
                onehot(order, b), feat[b], TN, preferred_element_type=F32
            ).astype(BF)
        halo(0, c).start()
        halo(1, c).start()

    for load in loads[2:5]:
        load.wait()

    def weight(i, j):
        who = (me.rep_sib, me.rep_y, me.rep_far)[i]
        src = (w_rel, w_root)[j]
        return remote(
            src.at[pl.ds(who * width, width)], slab.at[me.rep, pl.ds(j * width, width)],
            ws.at[i, j], wr.at[i, j], me.at_rep(who),
        )

    for i in range(3):
        for j in range(2):
            weight(i, j).start()
    for j, src in enumerate((w_rel, w_root)):
        slab[me.rep, j * width : (j + 1) * width] = src[pl.ds(me.rep * width, width), :]

    place_of = lax.broadcasted_iota(jnp.int32, (1, entries), 1)

    def collect(b, row):
        for k in range(per_row):
            row = jnp.where(place_of == b * per_row + k, cols[b, k], row)
        return row

    cols_row = lax.fori_loop(0, blocks, collect, jnp.zeros((1, entries), jnp.int32))
    sort_entries(cols_row, me, blocks, meta)
    meta_copy = pltpu.make_async_copy(meta, meta_s, meta_sem)
    meta_copy.start()

    @pl.loop(0, nc + 2)
    def _(s):
        @pl.when(s < nc)
        def _():
            halo(0, s).wait_recv()
            halo(1, s).wait_recv()
            halo(2, s).start()
            halo(3, s).start()
            halo(4, s).start()

        @pl.when(s >= 2)
        def _():
            halo(3, s - 2).wait_recv()
            halo(5, s - 2).start()

    @pl.loop(0, nc)
    def _(c):
        for kind in (2, 4, 5):
            halo(kind, c).wait_recv()

    for i in range(3):
        for j in range(2):
            weight(i, j).wait_recv()
    tile_copy.wait()
    loads[5].wait()
    meta_copy.wait()

    panel_sib = [2 * (1 - me.low) + 1 - me.core, 2 * me.low + 1 - me.core]
    panel_mine = [me.rep_y, me.rep]

    def rows(c):
        return pl.ds(c * mb, mb)

    def mid(kind, c):
        src, dst, who = [
            (s1.at[c], r1.at[c], sib),
            (s2.at[c], r2.at[c], far_y),
            (pre.at[me.rep, rows(c)], pre.at[me.rep, rows(c)], far_y),
            (pre.at[me.rep, rows(c)], pre.at[me.rep, rows(c)], sib),
            (pre.at[me.rep_y, rows(c)], pre.at[me.rep_y, rows(c)], sib),
        ][kind]
        return remote(src, dst, ms.at[kind, c], mr.at[kind, c], who)

    def both(c):
        return jnp.concatenate(
            [
                agg[rows(c)].reshape(mrows, width),
                win[pl.ds(own + c * mb, mb)].reshape(mrows, width),
            ],
            axis=1,
        )

    lag_b, lag_c, lag_d, lag_e = MID_LAGS

    @pl.loop(0, nm + lag_e)
    def _(s):
        @pl.when(s < nm)
        def _():
            for i in range(mb):
                b = s * mb + i
                left = jnp.concatenate([tbuf[b, k] for k in range(per_row)], axis=1)
                right = jnp.concatenate(
                    [win[slot_of(cols[b, k], me, blocks)] for k in range(per_row)], axis=0
                )
                agg[b] = jnp.dot(left, right, preferred_element_type=F32).astype(BF)
            x = both(s)
            for i in range(2):
                part = jnp.dot(x, slab[panel_sib[i]], preferred_element_type=F32)
                s1[s, i] = part.astype(BF)
            mid(0, s).start()
            for i in range(2):
                keep[s, i] = jnp.dot(x, slab[panel_mine[i]], preferred_element_type=F32)

        @pl.when((s >= lag_b) & (s < nm + lag_b))
        def _():
            c = s - lag_b
            mid(0, c).wait_recv()
            s2[c] = (keep[c, 0] + r1[c, 0].astype(F32)).astype(BF)
            mid(1, c).start()

        @pl.when((s >= lag_c) & (s < nm + lag_c))
        def _():
            c = s - lag_c
            mid(1, c).wait_recv()
            v = keep[c, 1] + r1[c, 1].astype(F32) + r2[c].astype(F32)
            sq = v * v
            t = jnp.tanh(0.7978845608 * (v + 0.044715 * (sq * v)))
            up = upstream[rows(c)].reshape(mrows, width).astype(F32)
            hidden[rows(c)] = (0.5 * v * (1.0 + t)).astype(BF).reshape(mb, bl, width)
            slope = 0.5 * (1.0 + t) + 0.5 * v * (1.0 - t * t) * (
                0.7978845608 * (1.0 + 0.134145 * sq)
            )
            pre[me.rep, rows(c)] = (up * slope).astype(BF).reshape(mb, bl, width)
            mid(2, c).start()
            mid(3, c).start()

        @pl.when((s >= lag_d) & (s < nm + lag_d))
        def _():
            mid(2, s - lag_d).wait_recv()
            mid(4, s - lag_d).start()

        @pl.when(s >= lag_e)
        def _():
            c = s - lag_e
            mid(3, c).wait_recv()
            mid(4, c).wait_recv()
            x = both(c)
            gathered = jnp.concatenate(
                [pre[p, rows(c)].reshape(mrows, width) for p in range(4)], axis=1
            )
            slabs = jnp.concatenate([slab[p] for p in range(4)], axis=1)
            back = lax.dot_general(slabs, gathered, NT, preferred_element_type=F32)
            for i in range(mb):
                cut = back[:, i * bl : (i + 1) * bl]
                b = c * mb + i
                back_root[b] = cut[width:]
                right = jnp.concatenate([tbuf[b, k] for k in range(per_row)], axis=1)
                res = jnp.dot(cut[:width].astype(BF), right, preferred_element_type=F32)
                for k in range(per_row):
                    prod[b * per_row + k] = res[:, k * bl : (k + 1) * bl]
            grads = lax.dot_general(x, gathered, TN, preferred_element_type=F32)

            @pl.when(c == 0)
            def _():
                for p in range(4):
                    wgrad[p] = grads[:, p * width : (p + 1) * width]

            @pl.when(c > 0)
            def _():
                for p in range(4):
                    wgrad[p] += grads[:, p * width : (p + 1) * width]

    na = BACK_CHUNKS
    ab = blocks // na
    rows_all = me.rows
    x_others = [me.n1, me.n2, me.diag]
    POST, DIAG, Q, PP, N2, N1 = range(6)

    def part(ref, slot, c):
        return ref.at[pl.ds(slot * blocks + c * ab, ab)]

    out = win
    @pl.loop(0, nc)
    def _(c):
        for kind in range(6):
            halo(kind, c).wait_send()

    def back(kind, c):
        _, who = [
            (POST, me.at_x(me.n2)),
            (DIAG, me.at_x(me.n1)),
            (Q, me.row_by(-me.step_q)),
            (PP, me.row_by(-me.step_p)),
            (N2, me.at_x(me.n2)),
            (N1, me.at_x(me.n1)),
        ][kind]
        return remote(part(out, kind, c), part(land, kind, c), bs.at[kind, c], br.at[kind, c], who)

    def got(kind, b):
        return land[kind * blocks + b].astype(F32)

    def local(slot, b):
        at = slot * blocks + b
        last = meta_s[2, at]
        return tbuf[lax.div(last, per_row), lax.rem(last, per_row)].astype(F32) * meta_s[3, at].astype(F32)

    alone = me.x == me.rep

    def give(p):
        return remote(
            wsend.at[p], a1.at[me.x], e0s.at[p], e0r.at[me.x], (me.row * ROW + me.rep, p)
        )

    def take(x):
        return remote(wsend.at[0], a1.at[x], e0s.at[0], e0r.at[x], (me.row * ROW + x, me.x))

    def unless_self(i, mine, act):
        @pl.when(jnp.logical_not(alone & (mine == i)))
        def _():
            act(i)

    def scatter_rows(d):
        who = lax.rem(me.row + d, rows_all)
        return remote(piece.at[who], a2.at[d], e2s.at[d], e2r.at[d], me.at_row(who))

    def gather_rows(d):
        who = lax.rem(me.row + d, rows_all)
        return remote(done, a3.at[me.row], e3s.at[d], e3r.at[d], me.at_row(who))

    def gather_x(i):
        return remote(a3, a4.at[me.x], e4s.at[i], e4r.at[i], me.at_x(x_others[i]))

    for p in range(4):
        wsend[p] = wgrad[p].astype(BF)
    for p in range(4):
        unless_self(p, me.rep, lambda i: give(i).start())

    @pl.when(alone)
    def _():
        a1[me.x] = wsend[me.rep]

    def add(e, total):
        total = total * meta_s[1, e].astype(F32) + prod[meta_s[0, e]]
        tbuf[lax.div(e, per_row), lax.rem(e, per_row)] = total.astype(BF)
        return total

    lax.fori_loop(0, entries, add, jnp.zeros((width, bl), F32), unroll=8)
    lag_p, lag_n, lag_out = BACK_LAGS

    @pl.loop(0, na + lag_out)
    def _(s):
        @pl.when(s < na)
        def _():
            c = s
            for kind, slot in ((POST, me.slot_post), (DIAG, me.slot_diag), (Q, me.slot_q)):
                for i in range(ab):
                    b = c * ab + i
                    out[kind * blocks + b] = local(slot, b).astype(BF)
                back(kind, c).start()

        @pl.when((s >= lag_p) & (s < na + lag_p))
        def _():
            c = s - lag_p
            back(POST, c).wait_recv()
            for i in range(ab):
                b = c * ab + i
                out[PP * blocks + b] = (local(me.slot_p, b) + got(POST, b)).astype(BF)
            back(PP, c).start()

        @pl.when((s >= lag_n) & (s < na + lag_n))
        def _():
            c = s - lag_n
            back(DIAG, c).wait_recv()
            back(Q, c).wait_recv()
            for i in range(ab):
                b = c * ab + i
                out[N2 * blocks + b] = (local(me.slot_n2, b) + got(DIAG, b) + got(Q, b)).astype(BF)
            back(N2, c).start()

        @pl.when((s >= lag_n) & (s < na + lag_n))
        def _():
            c = s - lag_n
            back(PP, c).wait_recv()
            for i in range(ab):
                b = c * ab + i
                out[N1 * blocks + b] = (local(me.slot_n1, b) + got(PP, b)).astype(BF)
            back(N1, c).start()

        @pl.when(s == WGRAD_STEPS[0])
        def _():
            for x in range(4):
                unless_self(x, me.x, lambda i: take(i).wait_recv())
            summed = a1[0].astype(F32)
            for x in range(1, 4):
                summed += a1[x].astype(F32)
            piece[...] = summed.reshape(piece.shape)
            for d in range(1, rows_all):
                scatter_rows(d).start()

        @pl.when(s == WGRAD_STEPS[1])
        def _():
            for d in range(1, rows_all):
                scatter_rows(d).wait_recv()
            total = piece[me.row]
            for d in range(1, rows_all):
                total += a2[d]
            done[...] = total.astype(BF)
            a3[me.row] = total.astype(BF)
            for d in range(1, rows_all):
                gather_rows(d).start()

        @pl.when(s == WGRAD_STEPS[2])
        def _():
            for d in range(1, rows_all):
                gather_rows(d).wait_recv()
            for i in range(3):
                gather_x(i).start()
            a4[me.x] = a3[...]

        @pl.when(s >= lag_out)
        def _():
            c = s - lag_out
            back(N2, c).wait_recv()
            back(N1, c).wait_recv()
            for i in range(ab):
                b = c * ab + i
                total = local(REACH, b) + back_root[b] + got(N1, b) + got(N2, b)
                grad_feat[b] = lax.dot_general(
                    onehot(order, b), total.astype(BF), NT, preferred_element_type=F32
                ).astype(BF)

    for i in range(3):
        gather_x(i).wait_recv()
    for p in range(4):
        both = a4[p].reshape(2 * width, width).astype(F32)
        grad_rel[p * width : (p + 1) * width, :] = both[:width]
        grad_root[p * width : (p + 1) * width, :] = both[width:]

    @pl.loop(0, na)
    def _(c):
        for kind in range(6):
            back(kind, c).wait_send()

    for i in range(3):
        gather_x(i).wait_send()
    for p in range(4):
        unless_self(p, me.rep, lambda i: give(i).wait_send())
    for d in range(1, rows_all):
        scatter_rows(d).wait_send()
        gather_rows(d).wait_send()

    @pl.loop(0, nm)
    def _(c):
        for kind in range(5):
            mid(kind, c).wait_send()

    for i in range(3):
        for j in range(2):
            weight(i, j).wait_send()


def on_device(features, order, columns, tiles, w_rel, w_root, upstream):
    groups = lax.axis_size("blk")
    blocks, bl = order.shape
    width = features.shape[1]
    rows = groups // ROW
    vmem = pl.BlockSpec(memory_space=pltpu.VMEM)
    hbm = pl.BlockSpec(memory_space=pltpu.HBM)
    dma = pltpu.SemaphoreType.DMA
    cube = (blocks, bl, width)
    mrows = blocks // MID_CHUNKS * bl

    def shape(dims, dtype):
        return jax.ShapeDtypeStruct(dims, dtype)

    piece = (2 * width // rows, width)
    entries = columns.size
    hidden, grad_feat, grad_rel, grad_root = pl.pallas_call(
        lambda *refs: layer_kernel(groups, *refs),
        out_shape=(
            shape(cube, BF),
            shape(cube, BF),
            shape((4 * width, width), F32),
            shape((4 * width, width), F32),
        ),
        in_specs=[hbm] * 7,
        out_specs=(vmem,) * 4,
        scratch_shapes=[
            pltpu.SMEM(columns.shape, jnp.int32),
            pltpu.VMEM(cube, BF),
            pltpu.VMEM(order.shape, jnp.int32),
            pltpu.VMEM(w_rel.shape, BF),
            pltpu.VMEM(w_root.shape, BF),
            pltpu.VMEM(cube, BF),
            pltpu.VMEM((SPAN * blocks, bl, width), BF),
            pltpu.VMEM(tiles.shape, BF),
            pltpu.VMEM(cube, BF),
            pltpu.VMEM((4, 2 * width, width), BF),
            pltpu.VMEM((MID_CHUNKS, 2, mrows, width), F32),
            pltpu.VMEM((MID_CHUNKS, 2, mrows, width), BF),
            pltpu.VMEM((MID_CHUNKS, 2, mrows, width), BF),
            pltpu.VMEM((MID_CHUNKS, mrows, width), BF),
            pltpu.VMEM((MID_CHUNKS, mrows, width), BF),
            pltpu.VMEM((4,) + cube, BF),
            pltpu.VMEM((blocks, width, bl), F32),
            pltpu.VMEM((4, 2 * width, width), F32),
            pltpu.VMEM((entries, width, bl), F32),
            pltpu.VMEM((8, entries), jnp.int32),
            pltpu.SMEM((8, entries), jnp.int32),
            pltpu.VMEM((6 * blocks, width, bl), BF),
            pltpu.VMEM((4, 2 * width, width), BF),
            pltpu.VMEM((4, 2 * width, width), BF),
            pltpu.VMEM((rows,) + piece, F32),
            pltpu.VMEM((rows,) + piece, BF),
            pltpu.VMEM((4, rows) + piece, BF),
            pltpu.VMEM((rows,) + piece, F32),
            pltpu.VMEM(piece, BF),
            dma((6,)),
            dma(()),
            dma(()),
            dma((6, HALO_CHUNKS)),
            dma((6, HALO_CHUNKS)),
            dma((3, 2)),
            dma((3, 2)),
            dma((5, MID_CHUNKS)),
            dma((5, MID_CHUNKS)),
            dma((6, BACK_CHUNKS)),
            dma((6, BACK_CHUNKS)),
            dma((4,)), dma((4,)),
            dma((rows,)), dma((rows,)),
            dma((rows,)), dma((rows,)),
            dma((3,)), dma((3,)),
        ],
        compiler_params=pltpu.CompilerParams(
            collective_id=0, has_side_effects=True, vmem_limit_bytes=52 * MIB
        ),
        name="layer",
    )(
        columns, features.reshape(cube), order, tiles, w_rel, w_root,
        upstream.reshape(cube),
    )

    flat = (blocks * bl, width)
    return hidden.reshape(flat), grad_feat.reshape(flat), grad_rel, grad_root


def solution(mesh):
    in_specs = (
        P("blk", "rep"),
        P("blk", None),
        P("blk", None),
        P("blk", None, None, None),
        P(None, "rep"),
        P(None, "rep"),
        P("blk", "rep"),
    )
    out_specs = (P("blk", "rep"), P("blk", "rep"), P(None, "rep"), P(None, "rep"))
    return jax.shard_map(
        on_device, mesh=mesh, in_specs=in_specs, out_specs=out_specs, check_vma=False
    )
```

```python
import jax
import jax.numpy as jnp
from jax import lax
from jax.experimental import pallas as pl
from jax.experimental.pallas import tpu as pltpu
from jax.sharding import PartitionSpec as P

MESH = pl.DeviceIdType.MESH
REACH = 3
SPAN = 2 * REACH + 1
ROW = 4
HALO_CHUNKS = 4
MID_CHUNKS = 8
BACK_CHUNKS = 16
MID_LAGS = (1, 3, 5, 6)
BACK_LAGS = (2, 5, 8)
WGRAD_STEPS = (5, 11, 17)
BF = jnp.bfloat16
F32 = jnp.float32
NT = (((1,), (1,)), ((), ()))
TN = (((0,), (0,)), ((), ()))
MIB = 2**20


class Place:
    def __init__(self, groups):
        blk = lax.axis_index("blk")
        rep = lax.axis_index("rep")
        self.groups = groups
        self.rows = groups // ROW
        self.blk, self.rep = blk, rep
        x = lax.rem(blk, ROW)
        self.x = x
        self.row = lax.div(blk, ROW)
        half, odd = lax.div(x, 2), lax.rem(x, 2)
        self.n1 = 3 - x
        self.n2 = x + 1 - 2 * odd
        self.diag = lax.rem(x + 2, 4)
        self.step_p = 1 - 2 * half
        self.step_q = 1 - 2 * odd
        self.slot_n1 = REACH + self.n1 - x
        self.slot_n2 = REACH + self.n2 - x
        self.slot_diag = REACH + self.diag - x
        self.slot_p = REACH + self.n1 - x - ROW * self.step_p
        self.slot_q = REACH + self.n2 - x - ROW * self.step_q
        self.slot_post = 1 + 4 * half
        self.core = lax.rem(rep, 2)
        self.low = lax.div(rep, 2)
        self.rep_sib = 2 * self.low + 1 - self.core
        self.rep_y = 2 * (1 - self.low) + self.core
        self.rep_far = 2 * (1 - self.low) + 1 - self.core

    def at_x(self, x):
        return (self.row * ROW + x, self.rep)

    def at_row(self, row):
        return (row * ROW + self.x, self.rep)

    def row_by(self, step):
        return self.at_row(lax.rem(self.row + step + self.rows, self.rows))

    def near(self, d):
        at = lax.rem(self.x * 4 + self.rep + d, 16)
        return (self.row * ROW + lax.div(at, 4), lax.rem(at, 4))

    def at_rep(self, rep):
        return (self.blk, rep)


def greet(partners):
    barrier = pltpu.get_barrier_semaphore()
    for who in partners:
        pl.semaphore_signal(barrier, inc=1, device_id=who, device_id_type=MESH)
    pl.semaphore_wait(barrier, len(partners))


def remote(src, dst, send, recv, who):
    return pltpu.make_async_remote_copy(
        src_ref=src, dst_ref=dst, send_sem=send, recv_sem=recv, device_id=who, device_id_type=MESH
    )


def onehot(order_ref, b):
    length = order_ref.shape[1]
    node = lax.broadcasted_iota(jnp.int32, (length, length), 0)
    return (node == order_ref[pl.ds(b, 1), :]).astype(F32).astype(BF)


def slot_of(col, place, blocks):
    group = lax.shift_right_arithmetic(col, jnp.int32(blocks.bit_length() - 1))
    offset = (group - place.blk + REACH + place.groups) & (place.groups - 1)
    return jnp.minimum(offset, SPAN - 1) * blocks + (col & (blocks - 1))


def sort_entries(cols_row, place, blocks, meta):
    count = cols_row.shape[1]
    slot = slot_of(cols_row, place, blocks)
    entry = lax.broadcasted_iota(jnp.int32, (count, count), 1)
    slots = jnp.broadcast_to(slot, (count, count))
    slots_t = slots.T
    keys, keys_t = slots * count + entry, slots_t * count + entry.T
    earlier = (keys_t < keys).astype(jnp.int32)
    rank = jnp.sum(earlier, axis=0, keepdims=True)
    same = jnp.sum(jnp.where(slots_t == slots, earlier, 0), axis=0, keepdims=True)
    rank_t = jnp.broadcast_to(rank, (count, count)).T
    same_t = jnp.broadcast_to(same, (count, count)).T
    here = rank_t == entry
    meta[0:1, :] = jnp.sum(jnp.where(here, entry.T, 0), axis=0, keepdims=True)
    meta[1:2, :] = jnp.sum(jnp.where(here, jnp.minimum(same_t, 1), 0), axis=0, keepdims=True)
    upto = jnp.sum((slots_t <= entry).astype(jnp.int32), axis=0, keepdims=True)
    meta[2:3, :] = jnp.maximum(upto - 1, 0)
    found = jnp.sum((slots_t == entry).astype(jnp.int32), axis=0, keepdims=True)
    meta[3:4, :] = jnp.minimum(found, 1)


def layer_kernel(
    groups,
    cols_in, feat_in, order_in, tiles, w_rel_in, w_root_in, upstream_in,
    hidden, grad_feat, grad_rel, grad_root,
    cols, feat, order, w_rel, w_root, upstream, win, tbuf, agg, slab, keep, s1, r1, s2, r2, pre, back_root, wgrad, prod, meta, meta_s,
    land, wsend, a1, a2, a3, a4, piece, done,
    in_sem, tile_sem, meta_sem, hs, hr, ws, wr, ms, mr,
    bs, br, e0s, e0r, e2s, e2r, e3s, e3r, e4s, e4r,
):
    me = Place(groups)
    blocks, bl, width = feat.shape
    per_row = cols.shape[1]
    entries = blocks * per_row
    own = REACH * blocks
    nc = HALO_CHUNKS
    hb = blocks // nc
    nm = MID_CHUNKS
    mb = blocks // nm
    mrows = mb * bl

    loads = [
        pltpu.make_async_copy(src, dst, in_sem.at[i])
        for i, (src, dst) in enumerate(
            (
                (feat_in, feat),
                (order_in, order),
                (w_rel_in, w_rel),
                (w_root_in, w_root),
                (cols_in, cols),
                (upstream_in, upstream),
            )
        )
    ]
    for load in loads:
        load.start()
    tile_copy = pltpu.make_async_copy(tiles, tbuf, tile_sem)
    tile_copy.start()
    sib, far_y = me.at_rep(me.rep_sib), me.at_rep(me.rep_y)
    greet([me.near(d) for d in range(1, 16)] + [me.row_by(d) for d in range(1, me.rows)])

    loads[0].wait()
    loads[1].wait()

    def halo(kind, c):
        src_slot, dst_slot, who = [
            (REACH, REACH + me.x - me.n1, me.at_x(me.n1)),
            (REACH, REACH + me.x - me.n2, me.at_x(me.n2)),
            (me.slot_n2, REACH + me.n2 - me.n1, me.at_x(me.n1)),
            (me.slot_n1, me.slot_p, me.row_by(me.step_p)),
            (me.slot_n2, me.slot_q, me.row_by(me.step_q)),
            (me.slot_p, me.slot_post, me.at_x(me.n2)),
        ][kind]
        return remote(
            win.at[pl.ds(src_slot * blocks + c * hb, hb)],
            win.at[pl.ds(dst_slot * blocks + c * hb, hb)],
            hs.at[kind, c], hr.at[kind, c], who,
        )

    @pl.loop(0, nc)
    def _(c):
        for i in range(hb):
            b = c * hb + i
            win[own + b] = lax.dot_general(
                onehot(order, b), feat[b], TN, preferred_element_type=F32
            ).astype(BF)
        halo(0, c).start()
        halo(1, c).start()

    for load in loads[2:5]:
        load.wait()

    def weight(i, j):
        who = (me.rep_sib, me.rep_y, me.rep_far)[i]
        src = (w_rel, w_root)[j]
        return remote(
            src.at[pl.ds(who * width, width)], slab.at[me.rep, pl.ds(j * width, width)],
            ws.at[i, j], wr.at[i, j], me.at_rep(who),
        )

    for i in range(3):
        for j in range(2):
            weight(i, j).start()
    for j, src in enumerate((w_rel, w_root)):
        slab[me.rep, j * width : (j + 1) * width] = src[pl.ds(me.rep * width, width), :]

    place_of = lax.broadcasted_iota(jnp.int32, (1, entries), 1)

    def collect(b, row):
        for k in range(per_row):
            row = jnp.where(place_of == b * per_row + k, cols[b, k], row)
        return row

    cols_row = lax.fori_loop(0, blocks, collect, jnp.zeros((1, entries), jnp.int32))
    sort_entries(cols_row, me, blocks, meta)
    meta_copy = pltpu.make_async_copy(meta, meta_s, meta_sem)
    meta_copy.start()

    @pl.loop(0, nc + 2)
    def _(s):
        @pl.when(s < nc)
        def _():
            halo(0, s).wait_recv()
            halo(1, s).wait_recv()
            halo(3, s).start()
            halo(4, s).start()
            halo(2, s).start()

        @pl.when(s >= 2)
        def _():
            halo(3, s - 2).wait_recv()
            halo(5, s - 2).start()

    @pl.loop(0, nc)
    def _(c):
        for kind in (2, 4, 5):
            halo(kind, c).wait_recv()

    for i in range(3):
        for j in range(2):
            weight(i, j).wait_recv()
    tile_copy.wait()
    loads[5].wait()
    meta_copy.wait()

    panel_sib = [2 * (1 - me.low) + 1 - me.core, 2 * me.low + 1 - me.core]
    panel_mine = [me.rep_y, me.rep]

    def rows(c):
        return pl.ds(c * mb, mb)

    def mid(kind, c):
        src, dst, who = [
            (s1.at[c], r1.at[c], sib),
            (s2.at[c], r2.at[c], far_y),
            (pre.at[me.rep, rows(c)], pre.at[me.rep, rows(c)], far_y),
            (pre.at[me.rep, rows(c)], pre.at[me.rep, rows(c)], sib),
            (pre.at[me.rep_y, rows(c)], pre.at[me.rep_y, rows(c)], sib),
        ][kind]
        return remote(src, dst, ms.at[kind, c], mr.at[kind, c], who)

    def both(c):
        return jnp.concatenate(
            [
                agg[rows(c)].reshape(mrows, width),
                win[pl.ds(own + c * mb, mb)].reshape(mrows, width),
            ],
            axis=1,
        )

    lag_b, lag_c, lag_d, lag_e = MID_LAGS

    @pl.loop(0, nm + lag_e)
    def _(s):
        @pl.when(s < nm)
        def _():
            for i in range(mb):
                b = s * mb + i
                left = jnp.concatenate([tbuf[b, k] for k in range(per_row)], axis=1)
                right = jnp.concatenate(
                    [win[slot_of(cols[b, k], me, blocks)] for k in range(per_row)], axis=0
                )
                agg[b] = jnp.dot(left, right, preferred_element_type=F32).astype(BF)
            x = both(s)
            for i in range(2):
                part = jnp.dot(x, slab[panel_sib[i]], preferred_element_type=F32)
                s1[s, i] = part.astype(BF)
            mid(0, s).start()
            for i in range(2):
                keep[s, i] = jnp.dot(x, slab[panel_mine[i]], preferred_element_type=F32)

        @pl.when((s >= lag_b) & (s < nm + lag_b))
        def _():
            c = s - lag_b
            mid(0, c).wait_recv()
            s2[c] = (keep[c, 0] + r1[c, 0].astype(F32)).astype(BF)
            mid(1, c).start()

        @pl.when((s >= lag_c) & (s < nm + lag_c))
        def _():
            c = s - lag_c
            mid(1, c).wait_recv()
            v = keep[c, 1] + r1[c, 1].astype(F32) + r2[c].astype(F32)
            sq = v * v
            t = jnp.tanh(0.7978845608 * (v + 0.044715 * (sq * v)))
            up = upstream[rows(c)].reshape(mrows, width).astype(F32)
            hidden[rows(c)] = (0.5 * v * (1.0 + t)).astype(BF).reshape(mb, bl, width)
            slope = 0.5 * (1.0 + t) + 0.5 * v * (1.0 - t * t) * (
                0.7978845608 * (1.0 + 0.134145 * sq)
            )
            pre[me.rep, rows(c)] = (up * slope).astype(BF).reshape(mb, bl, width)
            mid(2, c).start()
            mid(3, c).start()

        @pl.when((s >= lag_d) & (s < nm + lag_d))
        def _():
            mid(2, s - lag_d).wait_recv()
            mid(4, s - lag_d).start()

        @pl.when(s >= lag_e)
        def _():
            c = s - lag_e
            mid(3, c).wait_recv()
            mid(4, c).wait_recv()
            x = both(c)
            gathered = jnp.concatenate(
                [pre[p, rows(c)].reshape(mrows, width) for p in range(4)], axis=1
            )
            slabs = jnp.concatenate([slab[p] for p in range(4)], axis=1)
            back = lax.dot_general(slabs, gathered, NT, preferred_element_type=F32)
            for i in range(mb):
                cut = back[:, i * bl : (i + 1) * bl]
                b = c * mb + i
                back_root[b] = cut[width:]
                right = jnp.concatenate([tbuf[b, k] for k in range(per_row)], axis=1)
                res = jnp.dot(cut[:width].astype(BF), right, preferred_element_type=F32)
                for k in range(per_row):
                    prod[b * per_row + k] = res[:, k * bl : (k + 1) * bl]
            grads = lax.dot_general(x, gathered, TN, preferred_element_type=F32)

            @pl.when(c == 0)
            def _():
                for p in range(4):
                    wgrad[p] = grads[:, p * width : (p + 1) * width]

            @pl.when(c > 0)
            def _():
                for p in range(4):
                    wgrad[p] += grads[:, p * width : (p + 1) * width]

    na = BACK_CHUNKS
    ab = blocks // na
    rows_all = me.rows
    x_others = [me.n1, me.n2, me.diag]
    POST, DIAG, Q, PP, N2, N1 = range(6)

    def part(ref, slot, c):
        return ref.at[pl.ds(slot * blocks + c * ab, ab)]

    out = win
    @pl.loop(0, nc)
    def _(c):
        for kind in range(6):
            halo(kind, c).wait_send()

    def back(kind, c):
        _, who = [
            (POST, me.at_x(me.n2)),
            (DIAG, me.at_x(me.n1)),
            (Q, me.row_by(-me.step_q)),
            (PP, me.row_by(-me.step_p)),
            (N2, me.at_x(me.n2)),
            (N1, me.at_x(me.n1)),
        ][kind]
        return remote(part(out, kind, c), part(land, kind, c), bs.at[kind, c], br.at[kind, c], who)

    def got(kind, b):
        return land[kind * blocks + b].astype(F32)

    def local(slot, b):
        at = slot * blocks + b
        last = meta_s[2, at]
        return tbuf[lax.div(last, per_row), lax.rem(last, per_row)].astype(F32) * meta_s[3, at].astype(F32)

    alone = me.x == me.rep

    def give(p):
        return remote(
            wsend.at[p], a1.at[me.x], e0s.at[p], e0r.at[me.x], (me.row * ROW + me.rep, p)
        )

    def take(x):
        return remote(wsend.at[0], a1.at[x], e0s.at[0], e0r.at[x], (me.row * ROW + x, me.x))

    def unless_self(i, mine, act):
        @pl.when(jnp.logical_not(alone & (mine == i)))
        def _():
            act(i)

    def scatter_rows(d):
        who = lax.rem(me.row + d, rows_all)
        return remote(piece.at[who], a2.at[d], e2s.at[d], e2r.at[d], me.at_row(who))

    def gather_rows(d):
        who = lax.rem(me.row + d, rows_all)
        return remote(done, a3.at[me.row], e3s.at[d], e3r.at[d], me.at_row(who))

    def gather_x(i):
        return remote(a3, a4.at[me.x], e4s.at[i], e4r.at[i], me.at_x(x_others[i]))

    for p in range(4):
        wsend[p] = wgrad[p].astype(BF)
    for p in range(4):
        unless_self(p, me.rep, lambda i: give(i).start())

    @pl.when(alone)
    def _():
        a1[me.x] = wsend[me.rep]

    def add(e, total):
        total = total * meta_s[1, e].astype(F32) + prod[meta_s[0, e]]
        tbuf[lax.div(e, per_row), lax.rem(e, per_row)] = total.astype(BF)
        return total

    lax.fori_loop(0, entries, add, jnp.zeros((width, bl), F32), unroll=8)
    lag_p, lag_n, lag_out = BACK_LAGS

    @pl.loop(0, na + lag_out)
    def _(s):
        @pl.when(s < na)
        def _():
            c = s
            for kind, slot in ((POST, me.slot_post), (DIAG, me.slot_diag), (Q, me.slot_q)):
                for i in range(ab):
                    b = c * ab + i
                    out[kind * blocks + b] = local(slot, b).astype(BF)
                back(kind, c).start()

        @pl.when((s >= lag_p) & (s < na + lag_p))
        def _():
            c = s - lag_p
            back(POST, c).wait_recv()
            for i in range(ab):
                b = c * ab + i
                out[PP * blocks + b] = (local(me.slot_p, b) + got(POST, b)).astype(BF)
            back(PP, c).start()

        @pl.when((s >= lag_n) & (s < na + lag_n))
        def _():
            c = s - lag_n
            back(DIAG, c).wait_recv()
            back(Q, c).wait_recv()
            for i in range(ab):
                b = c * ab + i
                out[N2 * blocks + b] = (local(me.slot_n2, b) + got(DIAG, b) + got(Q, b)).astype(BF)
            back(N2, c).start()

        @pl.when((s >= lag_n) & (s < na + lag_n))
        def _():
            c = s - lag_n
            back(PP, c).wait_recv()
            for i in range(ab):
                b = c * ab + i
                out[N1 * blocks + b] = (local(me.slot_n1, b) + got(PP, b)).astype(BF)
            back(N1, c).start()

        @pl.when(s == WGRAD_STEPS[0])
        def _():
            for x in range(4):
                unless_self(x, me.x, lambda i: take(i).wait_recv())
            summed = a1[0].astype(F32)
            for x in range(1, 4):
                summed += a1[x].astype(F32)
            piece[...] = summed.reshape(piece.shape)
            for d in range(1, rows_all):
                scatter_rows(d).start()

        @pl.when(s == WGRAD_STEPS[1])
        def _():
            for d in range(1, rows_all):
                scatter_rows(d).wait_recv()
            total = piece[me.row]
            for d in range(1, rows_all):
                total += a2[d]
            done[...] = total.astype(BF)
            a3[me.row] = total.astype(BF)
            for d in range(1, rows_all):
                gather_rows(d).start()

        @pl.when(s == WGRAD_STEPS[2])
        def _():
            for d in range(1, rows_all):
                gather_rows(d).wait_recv()
            for i in range(3):
                gather_x(i).start()
            a4[me.x] = a3[...]

        @pl.when(s >= lag_out)
        def _():
            c = s - lag_out
            back(N2, c).wait_recv()
            back(N1, c).wait_recv()
            for i in range(ab):
                b = c * ab + i
                total = local(REACH, b) + back_root[b] + got(N1, b) + got(N2, b)
                grad_feat[b] = lax.dot_general(
                    onehot(order, b), total.astype(BF), NT, preferred_element_type=F32
                ).astype(BF)

    for i in range(3):
        gather_x(i).wait_recv()
    for p in range(4):
        both = a4[p].reshape(2 * width, width).astype(F32)
        grad_rel[p * width : (p + 1) * width, :] = both[:width]
        grad_root[p * width : (p + 1) * width, :] = both[width:]

    @pl.loop(0, na)
    def _(c):
        for kind in range(6):
            back(kind, c).wait_send()

    for i in range(3):
        gather_x(i).wait_send()
    for p in range(4):
        unless_self(p, me.rep, lambda i: give(i).wait_send())
    for d in range(1, rows_all):
        scatter_rows(d).wait_send()
        gather_rows(d).wait_send()

    @pl.loop(0, nm)
    def _(c):
        for kind in range(5):
            mid(kind, c).wait_send()

    for i in range(3):
        for j in range(2):
            weight(i, j).wait_send()


def on_device(features, order, columns, tiles, w_rel, w_root, upstream):
    groups = lax.axis_size("blk")
    blocks, bl = order.shape
    width = features.shape[1]
    rows = groups // ROW
    vmem = pl.BlockSpec(memory_space=pltpu.VMEM)
    hbm = pl.BlockSpec(memory_space=pltpu.HBM)
    dma = pltpu.SemaphoreType.DMA
    cube = (blocks, bl, width)
    mrows = blocks // MID_CHUNKS * bl

    def shape(dims, dtype):
        return jax.ShapeDtypeStruct(dims, dtype)

    piece = (2 * width // rows, width)
    entries = columns.size
    hidden, grad_feat, grad_rel, grad_root = pl.pallas_call(
        lambda *refs: layer_kernel(groups, *refs),
        out_shape=(
            shape(cube, BF),
            shape(cube, BF),
            shape((4 * width, width), F32),
            shape((4 * width, width), F32),
        ),
        in_specs=[hbm] * 7,
        out_specs=(vmem,) * 4,
        scratch_shapes=[
            pltpu.SMEM(columns.shape, jnp.int32),
            pltpu.VMEM(cube, BF),
            pltpu.VMEM(order.shape, jnp.int32),
            pltpu.VMEM(w_rel.shape, BF),
            pltpu.VMEM(w_root.shape, BF),
            pltpu.VMEM(cube, BF),
            pltpu.VMEM((SPAN * blocks, bl, width), BF),
            pltpu.VMEM(tiles.shape, BF),
            pltpu.VMEM(cube, BF),
            pltpu.VMEM((4, 2 * width, width), BF),
            pltpu.VMEM((MID_CHUNKS, 2, mrows, width), F32),
            pltpu.VMEM((MID_CHUNKS, 2, mrows, width), BF),
            pltpu.VMEM((MID_CHUNKS, 2, mrows, width), BF),
            pltpu.VMEM((MID_CHUNKS, mrows, width), BF),
            pltpu.VMEM((MID_CHUNKS, mrows, width), BF),
            pltpu.VMEM((4,) + cube, BF),
            pltpu.VMEM((blocks, width, bl), F32),
            pltpu.VMEM((4, 2 * width, width), F32),
            pltpu.VMEM((entries, width, bl), F32),
            pltpu.VMEM((8, entries), jnp.int32),
            pltpu.SMEM((8, entries), jnp.int32),
            pltpu.VMEM((6 * blocks, width, bl), BF),
            pltpu.VMEM((4, 2 * width, width), BF),
            pltpu.VMEM((4, 2 * width, width), BF),
            pltpu.VMEM((rows,) + piece, F32),
            pltpu.VMEM((rows,) + piece, BF),
            pltpu.VMEM((4, rows) + piece, BF),
            pltpu.VMEM((rows,) + piece, F32),
            pltpu.VMEM(piece, BF),
            dma((6,)),
            dma(()),
            dma(()),
            dma((6, HALO_CHUNKS)),
            dma((6, HALO_CHUNKS)),
            dma((3, 2)),
            dma((3, 2)),
            dma((5, MID_CHUNKS)),
            dma((5, MID_CHUNKS)),
            dma((6, BACK_CHUNKS)),
            dma((6, BACK_CHUNKS)),
            dma((4,)), dma((4,)),
            dma((rows,)), dma((rows,)),
            dma((rows,)), dma((rows,)),
            dma((3,)), dma((3,)),
        ],
        compiler_params=pltpu.CompilerParams(
            collective_id=0, has_side_effects=True, vmem_limit_bytes=52 * MIB
        ),
        name="layer",
    )(
        columns, features.reshape(cube), order, tiles, w_rel, w_root,
        upstream.reshape(cube),
    )

    flat = (blocks * bl, width)
    return hidden.reshape(flat), grad_feat.reshape(flat), grad_rel, grad_root


def solution(mesh):
    in_specs = (
        P("blk", "rep"),
        P("blk", None),
        P("blk", None),
        P("blk", None, None, None),
        P(None, "rep"),
        P(None, "rep"),
        P("blk", "rep"),
    )
    out_specs = (P("blk", "rep"), P("blk", "rep"), P(None, "rep"), P(None, "rep"))
    return jax.shard_map(
        on_device, mesh=mesh, in_specs=in_specs, out_specs=out_specs, check_vma=False
    )
```
